128 devices in a mesh: tour: 64 (over y, z_lo, x, core), feat: 2 (over z_hi).
Axes of the slice: x: 4, y: 4, z: 4 (z_hi: 2, z_lo: 2; z = z_hi * 2 + z_lo), core: 2. Of those that a mesh axis runs over, the one named last changes fastest.
Arguments:
- projected: bfloat16 [32768, 1024], P('tour', 'feat'), may hold values from -220 to 220
- sharpness: float32 [], replicated, may hold values from 5 to 250
- partners: int32 [8, 64], replicated, may hold values from 0 to 63, as said below
- positives: int32 [32768], P('tour'), may hold values from 0 to 32767, as said below
Outputs:
- row_loss: float32 [32768], P('tour')
- view_grad: float32 [32768, 1024], P('tour', 'feat')
The draws below stay inside these ranges and needn't reach their ends.
Inputs may be any that keep to these rules, and one draw needn't show every extreme that they name: For each round r there is one number m_r with partners[r, a] = a XOR m_r for every block a; m_r = M XOR s_r, where M is a nonzero multiple of 8 and s_0, ..., s_7 is an ordering of 0 to 7. positives pairs the views of each block of 512 views among themselves: positives_i lies in i's block, differs from i, and positives of positives_i is i.
All inputs are finite; a program needn't handle non-finite values.
Results may differ from the reference program's by a relative error of at most 0.008.
Values may be sent and summed in bfloat16 or wider, within the bound.
No kernel may reach another device: no remote copies, remote signals or barrier semaphores. Data moves between devices by JAX's collectives and lax.ppermute only.
A program may use at most 128 MiB of HBM per device.

```python
import math
import jax
import jax.numpy as jnp
from jax import lax

D = 1024
ROWS_DEV = 512
ROUNDS = 8
BLOCKS = 64
VIEWS = 32768


def draw_projected(key, part):
    key = jax.random.fold_in(key, 11)
    first_key = jax.random.fold_in(key, 0)
    return jnp.clip(jax.random.normal(first_key, (VIEWS, D), jnp.float32), -6.0, 6.0).astype(jnp.bfloat16)


def draw_sharpness(key, part):
    key = jax.random.fold_in(key, 12)
    return jnp.exp(jax.random.uniform(key, (), jnp.float32, math.log(5.0), math.log(20.0)))


def draw_partners(key, part):
    key = jax.random.fold_in(key, 13)
    mask_key, order_key = jax.random.split(key)
    first_mask = 8 * jax.random.randint(mask_key, (), 1, BLOCKS // 8, dtype=jnp.int32)
    low_order = jax.random.permutation(order_key, ROUNDS).astype(jnp.int32)
    round_masks = jnp.bitwise_xor(first_mask, low_order)
    return jnp.bitwise_xor(jnp.arange(BLOCKS, dtype=jnp.int32)[None, :], round_masks[:, None])


def draw_positives(key, part):
    key = jax.random.fold_in(key, 14)
    block_keys = jax.random.split(key, BLOCKS)
    shuffled = jax.vmap(lambda block_key: jax.random.permutation(block_key, ROWS_DEV))(block_keys).astype(jnp.int32)
    swapped = jnp.bitwise_xor(jnp.arange(ROWS_DEV, dtype=jnp.int32), 1)
    block_ids = jnp.arange(BLOCKS, dtype=jnp.int32)[:, None]
    local_pos = jnp.zeros((BLOCKS, ROWS_DEV), jnp.int32).at[block_ids, shuffled].set(shuffled[:, swapped])
    return (local_pos + block_ids * ROWS_DEV).reshape(VIEWS)


def setup_inputs(seed: int = 0) -> dict:
    splits = jax.random.split(jax.random.key(seed), 5)
    projected = draw_projected(jax.random.fold_in(splits[4], 71), 0)
    sharpness = draw_sharpness(jax.random.fold_in(splits[4], 71), 0)
    partners = draw_partners(jax.random.fold_in(splits[4], 71), 0)
    positives = draw_positives(jax.random.fold_in(splits[4], 71), 0)
    return dict(projected=projected, sharpness=sharpness, partners=partners, positives=positives)


EPSILON = 1e-06

def block_scores(block_index, embedded_blocks, partners, sharpness):
    chosen = jnp.concatenate([block_index[None], partners[:, block_index]]).astype(jnp.int32)
    key_blocks = embedded_blocks[chosen].astype(jnp.float32)
    queries = embedded_blocks[block_index].astype(jnp.float32)
    scores = sharpness * jnp.einsum('qd,rkd->rqk', queries, key_blocks, precision=lax.Precision.HIGHEST)
    row_ids = jnp.arange(ROWS_DEV, dtype=jnp.int32)
    self_hit = row_ids[:, None] == row_ids[None, :]
    scores = scores.at[0].set(jnp.where(self_hit, -jnp.inf, scores[0]))
    return (scores, key_blocks, chosen)

def reference(projected, sharpness, partners, positives):
    floats = projected.astype(jnp.float32)
    inverse = lax.rsqrt(lax.optimization_barrier(jnp.sum(floats * floats, -1)) + EPSILON)
    unit_rows = floats * inverse[:, None]
    embedded = unit_rows.astype(jnp.bfloat16)
    embedded_blocks = embedded.reshape(BLOCKS, ROWS_DEV, D)
    starts = jnp.arange(BLOCKS, dtype=jnp.int32) * ROWS_DEV
    local_pos = positives.reshape(BLOCKS, ROWS_DEV) - starts[:, None]
    row_ids = jnp.arange(ROWS_DEV, dtype=jnp.int32)

    def forward_block(block_index):
        scores, key_blocks, chosen = block_scores(block_index, embedded_blocks, partners, sharpness)
        row_peak = lax.optimization_barrier(jnp.max(scores, axis=(0, 2)))
        exp_total = lax.optimization_barrier(jnp.sum(jnp.exp(scores - row_peak[None, :, None]), axis=(0, 2)))
        lse_rows = row_peak + jnp.log(exp_total)
        pos_hit = row_ids[None, :] == local_pos[block_index][:, None]
        loss_rows = lse_rows - lax.optimization_barrier(jnp.sum(jnp.where(pos_hit, scores[0], 0.0), -1))
        return (lse_rows, loss_rows)
    lse_blocks, loss_blocks = lax.map(forward_block, jnp.arange(BLOCKS, dtype=jnp.int32))

    def backward_block(block_index):
        scores, key_blocks, chosen = block_scores(block_index, embedded_blocks, partners, sharpness)
        lse_own = lse_blocks[block_index]
        lse_keys = lse_blocks[chosen]
        pos_hit = (row_ids[None, :] == local_pos[block_index][:, None]).astype(jnp.float32)
        weight = jnp.exp(scores - lse_own[None, :, None]) + jnp.exp(scores - lse_keys[:, None, :])
        weight = weight.at[0].add(-2.0 * pos_hit)
        rounded = lax.optimization_barrier(weight.astype(jnp.bfloat16))
        return sharpness * jnp.einsum('rqk,rkd->qd', rounded.astype(jnp.float32), key_blocks, precision=lax.Precision.HIGHEST)
    unit_grad = lax.map(backward_block, jnp.arange(BLOCKS, dtype=jnp.int32)).reshape(VIEWS, D)
    radial = lax.optimization_barrier(jnp.sum(unit_rows * unit_grad, -1))
    view_grad = inverse[:, None] * (unit_grad - unit_rows * radial[:, None])
    return (loss_blocks.reshape(VIEWS), view_grad)
```

```python
import functools

import jax
import jax.numpy as jnp
from jax import lax
from jax.experimental import pallas as pl
from jax.experimental.pallas import tpu as pltpu
from jax.sharding import PartitionSpec as P

EPSILON = 1e-06
ROWS = 512
HALF = 256
WIDTH = 1024
FEAT = 1
CORE = 2
X = {0: 0, 1: 4, 2: 8, 3: 12}
VMEM_BYTES = 48 * 1024 * 1024
F32 = jnp.float32
BF16 = jnp.bfloat16


def swap(value, mask):
    count = lax.axis_size(("tour", "feat"))
    pairs = [(source, source ^ mask) for source in range(count)]
    return lax.ppermute(value, ("tour", "feat"), pairs)


def spec(space=pltpu.VMEM):
    return pl.BlockSpec(memory_space=space)


def call(body, out_shape, smem, vmem, scratch=(), flops=0, nbytes=0):
    return pl.pallas_call(
        body,
        out_shape=out_shape,
        in_specs=[spec(pltpu.SMEM)] * len(smem) + [spec()] * len(vmem),
        out_specs=jax.tree.map(lambda _: spec(), out_shape),
        scratch_shapes=list(scratch),
        compiler_params=pltpu.CompilerParams(vmem_limit_bytes=VMEM_BYTES),
        cost_estimate=pl.CostEstimate(flops=flops, bytes_accessed=nbytes, transcendentals=0),
    )(*smem, *vmem)


def f32(*shape):
    return jax.ShapeDtypeStruct(shape, F32)


def bf16(*shape):
    return jax.ShapeDtypeStruct(shape, BF16)


def row_inverse(left, right):
    total = jnp.sum(left * left + right * right, -1, keepdims=True)
    return lax.rsqrt(total + EPSILON)


def embed_rows(left_ref, right_ref, out_ref, step=128):
    width = left_ref.shape[1]
    for start in range(0, out_ref.shape[0], step):
        rows = pl.ds(start, step)
        left = left_ref[rows, :].astype(F32)
        right = right_ref[rows, :].astype(F32)
        inverse = row_inverse(left, right)
        out_ref[rows, :width] = (left * inverse).astype(BF16)
        out_ref[rows, width:] = (right * inverse).astype(BF16)


def to_lanes(column):
    return jnp.broadcast_to(column, (128, 128)).T[0:1, :]


def to_rows(lanes):
    return jnp.broadcast_to(lanes, (128, 128)).T


def log_add(values):
    peak = functools.reduce(jnp.maximum, values)
    return peak + jnp.log(functools.reduce(jnp.add, [jnp.exp(value - peak) for value in values]))


def products(queries, keys):
    return lax.dot_general(queries, keys, (((1,), (1,)), ((), ())), preferred_element_type=F32)


def column_lse(score_ref, peak):
    total = jnp.zeros((8, score_ref.shape[1]), F32)
    for start in range(0, ROWS, 128):
        part = jnp.exp(score_ref[pl.ds(start, 128), :] - peak)
        total = total + jnp.sum(part.reshape(16, 8, part.shape[1]), axis=0)
    return peak + jnp.log(jnp.sum(total, axis=0, keepdims=True))


def column_peak(score_ref):
    peak = jnp.max(score_ref[pl.ds(0, 128), :], axis=0, keepdims=True)
    for start in range(128, ROWS, 128):
        peak = jnp.maximum(peak, jnp.max(score_ref[pl.ds(start, 128), :], axis=0, keepdims=True))
    return peak


def own_kernel(place_ref, sharp_ref, left_ref, right_ref, pos_ref, emb_ref, score_ref, lse_ref, hit_ref):
    half = place_ref[0]
    embed_rows(left_ref, right_ref, emb_ref)
    mine = pl.ds(pl.multiple_of(half * HALF, HALF), HALF)
    score_ref[...] = products(emb_ref[...], emb_ref[mine, :]) * sharp_ref[0]
    columns = lax.broadcasted_iota(jnp.int32, (128, HALF), 1) + half * HALF
    rows = lax.broadcasted_iota(jnp.int32, (128, HALF), 0)
    pos = pos_ref[0:1, mine] - place_ref[1]
    hits = jnp.zeros((1, HALF), F32)
    for start in range(0, ROWS, 128):
        chunk = pl.ds(start, 128)
        part = score_ref[chunk, :]
        hits = hits + jnp.sum(jnp.where(rows + start == pos, part, 0.0), axis=0, keepdims=True)
        score_ref[chunk, :] = jnp.where(rows + start == columns, -jnp.inf, part)
    lse_ref[...] = column_lse(score_ref, column_peak(score_ref))
    hit_ref[...] = hits


def key_kernel(left_ref, right_ref, out_ref):
    embed_rows(left_ref, right_ref, out_ref)


def tiles_kernel(count, sharp_ref, emb_ref, *refs):
    keys, (score_ref, row_ref, column_ref) = refs[:count], refs[count:]
    for j in range(count):
        score_ref[j] = products(emb_ref[...], keys[j][...]) * sharp_ref[0]
    for j in range(count):
        tile = score_ref.at[j]
        column_ref[:, j * HALF : (j + 1) * HALF] = column_lse(tile, column_peak(tile))
    for start in range(0, ROWS, 128):
        chunk = pl.ds(start, 128)
        slabs = [(j, pl.ds(k, 128)) for j in range(count) for k in (0, 128)]
        peak = functools.reduce(jnp.maximum, [score_ref[j, chunk, k] for j, k in slabs])
        peak = jnp.max(peak, axis=1, keepdims=True)
        total = functools.reduce(jnp.add, [jnp.exp(score_ref[j, chunk, k] - peak) for j, k in slabs])
        total = jnp.sum(total, axis=1, keepdims=True)
        row_ref[:, start : start + 128] = to_lanes(peak + jnp.log(total))


def grad_kernel(
    start, count, place_ref, sharp_ref, lse_ref, column_ref, left_ref, right_ref, pos_ref, own_ref, emb_ref,
    *refs,
):
    scores, keys = refs[:count], refs[count : count + 2 * 4]
    near_ref, far_ref, weight_ref = refs[-3:]
    half = place_ref[0]
    rows_count = near_ref.shape[0]
    mine = pl.ds(pl.multiple_of(half * HALF, HALF), HALF)
    own_lse = lse_ref[0:1, mine]
    pos = pos_ref[0:1, mine] - place_ref[1]
    for offset in range(0, rows_count, 128):
        chunk = pl.ds(start + offset, 128)
        out = pl.ds(offset, 128)
        base = to_rows(lse_ref[0:1, start + offset : start + offset + 128])
        base = jnp.concatenate([base, base], axis=1)
        rows = lax.broadcasted_iota(jnp.int32, (128, HALF), 0) + (start + offset)
        part = own_ref[chunk, :]
        weight = jnp.exp(part - base) + jnp.exp(part - own_lse) - jnp.where(rows == pos, 2.0, 0.0)
        weight_ref[out, 0:HALF] = weight.astype(BF16)
        tile = 0
        for score_ref in scores:
            for j in range(score_ref.shape[0]):
                part = score_ref[j, chunk, :]
                column = column_ref[0:1, tile * HALF : (tile + 1) * HALF]
                weight = jnp.exp(part - base) + jnp.exp(part - column)
                tile += 1
                weight_ref[out, tile * HALF : (tile + 1) * HALF] = weight.astype(BF16)
    total = jnp.dot(weight_ref[:, 0:HALF], emb_ref[mine, :], preferred_element_type=F32)
    for j, key_ref in enumerate(keys):
        total = total + jnp.dot(
            weight_ref[:, (j + 1) * HALF : (j + 2) * HALF], key_ref[...], preferred_element_type=F32
        )
    total = total * sharp_ref[0]
    chunk = pl.ds(start, rows_count)
    left = left_ref[chunk, :].astype(F32)
    right = right_ref[chunk, :].astype(F32)
    inverse = row_inverse(left, right)
    width = left.shape[1]
    left, right = left * inverse, right * inverse
    near, far = total[:, :width], total[:, width:]
    radial = jnp.sum(left * near + right * far, -1, keepdims=True)
    near_ref[...] = inverse * (near - left * radial)
    far_ref[...] = (inverse * (far - right * radial)).astype(BF16)


def branch(mask, place, sharp, projected, pos):
    half = place[0]
    other = swap(projected, FEAT)
    straight = swap(lax.dynamic_slice_in_dim(projected, half * HALF, HALF, 0), mask)
    crossed = swap(lax.dynamic_slice_in_dim(projected, (1 - half) * HALF, HALF, 0), mask | FEAT)

    emb, own_scores, own_column, own_hit = call(
        own_kernel,
        (bf16(ROWS, WIDTH), f32(ROWS, HALF), f32(1, HALF), f32(1, HALF)),
        (place, sharp),
        (projected, other, pos),
        flops=2 * ROWS * HALF * WIDTH,
        nbytes=4 << 20,
    )
    first = call(key_kernel, bf16(HALF, WIDTH), (), (straight, crossed), nbytes=1 << 20)
    keys = [first] + [swap(first, X[d]) for d in (1, 3, 2)]
    keys += [swap(key, CORE) for key in keys]
    met_column = swap(own_column, mask)

    def tiles(chosen):
        return call(
            functools.partial(tiles_kernel, len(chosen)),
            (f32(len(chosen), ROWS, HALF), f32(1, ROWS), f32(1, len(chosen) * HALF)),
            (sharp,),
            (emb, *chosen),
            flops=2 * len(chosen) * ROWS * HALF * WIDTH,
            nbytes=len(chosen) << 20,
        )

    groups = [(0, 4), (1, 2, 5, 6), (3, 7)]
    order = [j for group in groups for j in group]
    tiled = [tiles([keys[j] for j in group]) for group in groups]

    row_part = log_add([t[1] for t in tiled])
    spread = jnp.concatenate([own_column, own_column], axis=1)
    here = (lax.broadcasted_iota(jnp.int32, (1, ROWS), 1) // HALF) == half
    row_part = jnp.where(here, log_add([row_part, spread]), row_part)
    hits = jnp.where(here, jnp.concatenate([own_hit, own_hit], axis=1), 0.0)
    sent = jnp.concatenate([row_part, hits], axis=0)
    back = swap(sent, FEAT)
    lse = log_add([row_part, back[0:1]])
    loss = lse - (hits + back[1:2])

    offsets = (0, 1, 3, 2)
    pieces = {}
    for group, t in zip(groups, tiled, strict=True):
        for at, j in enumerate(group):
            pieces[offsets[j % 4], j // 4] = t[2][:, at * HALF : (at + 1) * HALF]
    pieces[0, 0] = log_add([pieces[0, 0], met_column])
    column = jnp.concatenate(
        [jnp.concatenate([pieces[d, c] for d in range(4)], axis=1) for c in range(2)], axis=0
    )
    column = log_add([column, jnp.flip(swap(column, CORE), 0)])
    arrived = {d: swap(column, X[d]).reshape(2, 4, HALF) for d in (1, 2, 3)}
    arrived[0] = column.reshape(2, 4, HALF)
    column = log_add(
        [jnp.stack([arrived[d][:, j ^ d] for j in range(4)], axis=1) for d in range(4)]
    )
    column = jnp.concatenate([column[j // 4, offsets[j % 4]][None] for j in order], axis=1)

    near, far = [], []
    for start in (0, HALF):
        out = call(
            functools.partial(grad_kernel, start, len(tiled)),
            (f32(HALF, WIDTH // 2), bf16(HALF, WIDTH // 2)),
            (place, sharp),
            (lse, column, projected, other, pos, own_scores, emb, *[t[0] for t in tiled], *[keys[j] for j in order]),
            scratch=[pltpu.VMEM((HALF, 9 * HALF), BF16)],
            flops=2 * HALF * 9 * HALF * WIDTH,
            nbytes=10 << 20,
        )
        near.append(out[0])
        far.append(swap(out[1], FEAT))
    view_grad = jnp.concatenate([a + b.astype(F32) for a, b in zip(near, far, strict=True)], axis=0)
    return loss.reshape(ROWS), view_grad


def per_device(projected, sharpness, partners, positives):
    place = jnp.stack([lax.axis_index("feat"), lax.axis_index("tour") * ROWS]).astype(jnp.int32)
    group = jnp.right_shift(partners[0, 0], 3)
    branches = [functools.partial(branch, 16 * bits) for bits in range(1, 8)]
    return lax.switch(
        group - 1, branches, place, sharpness.reshape(1), projected, positives.reshape(1, ROWS)
    )


def solution(mesh):
    in_specs = (P("tour", "feat"), P(), P(), P("tour"))
    out_specs = (P("tour"), P("tour", "feat"))
    return jax.shard_map(
        per_device, mesh=mesh, in_specs=in_specs, out_specs=out_specs, check_vma=False
    )
```

```python
import functools

import jax
import jax.numpy as jnp
from jax import lax
from jax.experimental import pallas as pl
from jax.experimental.pallas import tpu as pltpu
from jax.sharding import PartitionSpec as P

EPSILON = 1e-06
ROWS = 512
HALF = 256
PIECE = 128
WIDTH = 1024
FEAT = 1
CORE = 2
X = {0: 0, 1: 4, 2: 8, 3: 12}
VMEM_BYTES = 24 * 1024 * 1024
F32 = jnp.float32
BF16 = jnp.bfloat16


def swap(value, mask):
    count = lax.axis_size(("tour", "feat"))
    pairs = [(source, source ^ mask) for source in range(count)]
    return lax.ppermute(value, ("tour", "feat"), pairs)


def spec(space=pltpu.VMEM):
    return pl.BlockSpec(memory_space=space)


def call(body, out_shape, smem, vmem, scratch=(), flops=0, nbytes=0):
    return pl.pallas_call(
        body,
        out_shape=out_shape,
        in_specs=[spec(pltpu.SMEM)] * len(smem) + [spec()] * len(vmem),
        out_specs=jax.tree.map(lambda _: spec(), out_shape),
        scratch_shapes=list(scratch),
        compiler_params=pltpu.CompilerParams(vmem_limit_bytes=VMEM_BYTES),
        cost_estimate=pl.CostEstimate(flops=1, bytes_accessed=1, transcendentals=0),
    )(*smem, *vmem)


def f32(*shape):
    return jax.ShapeDtypeStruct(shape, F32)


def bf16(*shape):
    return jax.ShapeDtypeStruct(shape, BF16)


def row_inverse(left, right):
    total = jnp.sum(left * left + right * right, -1, keepdims=True)
    return lax.rsqrt(total + EPSILON)


def embed_rows(left_ref, right_ref, out_ref, step=128):
    width = left_ref.shape[1]

    def chunk(index, carry):
        rows = pl.ds(pl.multiple_of(index * step, step), step)
        left = left_ref[rows, :].astype(F32)
        right = right_ref[rows, :].astype(F32)
        inverse = row_inverse(left, right)
        out_ref[rows, :width] = (left * inverse).astype(BF16)
        out_ref[rows, width:] = (right * inverse).astype(BF16)
        return carry

    lax.fori_loop(0, left_ref.shape[0] // step, chunk, 0)


def to_lanes(column):
    return jnp.broadcast_to(column, (128, 128)).T[0:1, :]


def to_rows(lanes):
    return jnp.broadcast_to(lanes, (128, 128)).T


def log_add(values):
    peak = functools.reduce(jnp.maximum, values)
    return peak + jnp.log(functools.reduce(jnp.add, [jnp.exp(value - peak) for value in values]))


def products(queries, keys):
    return lax.dot_general(queries, keys, (((1,), (1,)), ((), ())), preferred_element_type=F32)


def column_lse(score_ref, peak):
    total = jnp.zeros((8, score_ref.shape[1]), F32)
    for start in range(0, ROWS, 128):
        part = jnp.exp(score_ref[pl.ds(start, 128), :] - peak)
        total = total + jnp.sum(part.reshape(16, 8, part.shape[1]), axis=0)
    return peak + jnp.log(jnp.sum(total, axis=0, keepdims=True))


def column_peak(score_ref):
    peak = jnp.max(score_ref[pl.ds(0, 128), :], axis=0, keepdims=True)
    for start in range(128, ROWS, 128):
        peak = jnp.maximum(peak, jnp.max(score_ref[pl.ds(start, 128), :], axis=0, keepdims=True))
    return peak


def own_kernel(
    half_ref, block_ref, sharp_ref, left_ref, top_ref, bottom_ref, far_ref, pos_ref,
    emb_ref, other_ref, score_ref, lse_ref, hit_ref,
):
    half = half_ref[0]
    near = half * HALF
    for start, right_ref in ((near, top_ref), (near + PIECE, bottom_ref), (HALF - near, far_ref)):
        rows = pl.ds(pl.multiple_of(start, PIECE), right_ref.shape[0])
        embed_rows(left_ref.at[rows], right_ref, emb_ref.at[rows])
        other_ref[rows, :] = right_ref[...]
    mine = pl.ds(pl.multiple_of(half * HALF, HALF), HALF)
    score_ref[...] = products(emb_ref[...], emb_ref[mine, :]) * sharp_ref[0]
    columns = lax.broadcasted_iota(jnp.int32, (128, HALF), 1) + half * HALF
    rows = lax.broadcasted_iota(jnp.int32, (128, HALF), 0)
    pos = pos_ref[0:1, mine] - block_ref[0]
    hits = jnp.zeros((1, HALF), F32)
    for start in range(0, ROWS, 128):
        chunk = pl.ds(start, 128)
        part = score_ref[chunk, :]
        hits = hits + jnp.sum(jnp.where(rows + start == pos, part, 0.0), axis=0, keepdims=True)
        score_ref[chunk, :] = jnp.where(rows + start == columns, -jnp.inf, part)
    lse_ref[...] = column_lse(score_ref, column_peak(score_ref))
    hit_ref[...] = hits


def prep_kernel(half_ref, partner_ref, whole_ref, group_ref, near_ref, top_ref, bottom_ref, met_ref, sems):
    near = half_ref[0] * HALF
    far = HALF - near
    copies = [
        pltpu.make_async_copy(
            whole_ref.at[pl.ds(pl.multiple_of(start, PIECE), out_ref.shape[0]), :], out_ref, sems.at[j]
        )
        for j, (start, out_ref) in enumerate(((far, top_ref), (far + PIECE, bottom_ref), (near, near_ref)))
    ]
    copies.append(pltpu.make_async_copy(partner_ref, met_ref, sems.at[3]))
    for copy in copies:
        copy.start()
    for copy in copies:
        copy.wait()
    group_ref[0] = jnp.right_shift(met_ref[0, 0], 3) - 1


def key_kernel(start, left_ref, right_ref, out_ref):
    embed_rows(left_ref.at[pl.ds(start, PIECE)], right_ref, out_ref)


def joined(refs):
    return refs[0][...] if len(refs) == 1 else jnp.concatenate([ref[...] for ref in refs], axis=0)


def tiles_kernel(sharp_ref, emb_ref, *refs):
    count = 2
    score_ref, row_ref, column_ref, key_ref = refs[-4:]
    for j in range(count):
        key_ref[j] = joined(refs[2 * j : 2 * j + 2])
        score_ref[j] = products(emb_ref[...], key_ref[j]) * sharp_ref[0]
    for j in range(count):
        tile = score_ref.at[j]
        column_ref[j : j + 1, :] = column_lse(tile, column_peak(tile))
    for start in range(0, ROWS, 128):
        chunk = pl.ds(start, 128)
        slabs = [(j, pl.ds(k, 128)) for j in range(count) for k in (0, 128)]
        peak = functools.reduce(jnp.maximum, [score_ref[j, chunk, k] for j, k in slabs])
        peak = jnp.max(peak, axis=1, keepdims=True)
        total = functools.reduce(jnp.add, [jnp.exp(score_ref[j, chunk, k] - peak) for j, k in slabs])
        total = jnp.sum(total, axis=1, keepdims=True)
        row_ref[:, start : start + 128] = to_lanes(peak + jnp.log(total))


GROUPS = (((0, 0), (0, 1)), ((1, 0), (3, 1)), ((3, 0), (1, 1)), ((2, 0), (2, 1)))
PLACES = {name: 2 * g + p for g, group in enumerate(GROUPS) for p, name in enumerate(group)}


def grad_kernel(start, *refs):
    half_ref, block_ref, sharp_ref, sent_ref, back_ref = refs[:5]
    column_ref, left_ref, right_ref, pos_ref, own_ref, emb_ref = refs[5:11]
    score_refs = refs[11:15]
    key_refs = refs[15:19]
    near_ref, far_ref, loss_ref, weight_ref, lse_ref = refs[19:]
    half = half_ref[0]
    rows_count = near_ref.shape[0]
    mine = pl.ds(pl.multiple_of(half * HALF, HALF), HALF)
    lse_ref[...] = log_add([sent_ref[0:1, :], back_ref[0:1, :]])
    loss = lse_ref[...] - (sent_ref[1:2, :] + back_ref[1:2, :])
    loss_ref[...] = loss[:, start : start + rows_count]
    own_lse = lse_ref[0:1, mine]
    pos = pos_ref[0:1, mine] - block_ref[0]
    for offset in range(0, rows_count, 128):
        chunk = pl.ds(start + offset, 128)
        out = pl.ds(offset, 128)
        base = to_rows(lse_ref[0:1, start + offset : start + offset + 128])
        base = jnp.concatenate([base, base], axis=1)
        rows = lax.broadcasted_iota(jnp.int32, (128, HALF), 0) + (start + offset)
        part = own_ref[chunk, :]
        weight = jnp.exp(part - base) + jnp.exp(part - own_lse) - jnp.where(rows == pos, 2.0, 0.0)
        weight_ref[out, 0:HALF] = weight.astype(BF16)
        for g in range(4):
            for core in range(2):
                tile = 1 + 2 * g + core
                part = score_refs[g][core, chunk, :]
                column = column_ref[core : core + 1, g * HALF : (g + 1) * HALF]
                weight = jnp.exp(part - base) + jnp.exp(part - column)
                weight_ref[out, tile * HALF : (tile + 1) * HALF] = weight.astype(BF16)
    total = jnp.dot(weight_ref[:, 0:HALF], emb_ref[mine, :], preferred_element_type=F32)
    for tile in range(8):
        key = key_refs[tile // 2][tile % 2]
        total = total + jnp.dot(
            weight_ref[:, (tile + 1) * HALF : (tile + 2) * HALF], key, preferred_element_type=F32
        )
    total = total * sharp_ref[0]
    chunk = pl.ds(start, rows_count)
    left = left_ref[chunk, :].astype(F32)
    right = right_ref[chunk, :].astype(F32)
    inverse = row_inverse(left, right)
    width = left.shape[1]
    left, right = left * inverse, right * inverse
    near, far = total[:, :width], total[:, width:]
    radial = jnp.sum(left * near + right * far, -1, keepdims=True)
    near_ref[...] = inverse * (near - left * radial)
    far_ref[...] = (inverse * (far - right * radial)).astype(BF16)


def exchange(mask, half, block, sharp, projected, pos, near_rows, far_top, far_bottom):
    arrived = [swap(rows, FEAT) for rows in (far_top, far_bottom, near_rows)]
    keys = [
        call(functools.partial(key_kernel, start), bf16(PIECE, WIDTH), (), (near_rows, rows))
        for start, rows in zip((0, PIECE), arrived)
    ]
    met = [swap(key, mask) for key in keys]
    emb, other, own_scores, own_column, own_hit = call(
        own_kernel,
        (bf16(ROWS, WIDTH), bf16(ROWS, WIDTH // 2), f32(ROWS, HALF), f32(1, HALF), f32(1, HALF)),
        (half, block, sharp),
        (projected, *arrived, pos),
    )
    return (*met, swap(own_column, mask), emb, other, own_scores, own_column, own_hit)


def after(value, *done):
    return lax.optimization_barrier((value, *done))[0]


def shifted(columns, offset):
    at = [PLACES[name[0] ^ offset, name[1]] * PIECE for group in GROUPS for name in group]
    return jnp.concatenate([columns[:, start : start + PIECE] for start in at], axis=1)


def per_device(projected, sharpness, partners, positives):
    half = lax.axis_index("feat").astype(jnp.int32)
    block = (lax.axis_index("tour") * ROWS).astype(jnp.int32)
    place = (half.reshape(1), block.reshape(1))
    sharp = sharpness.reshape(1)
    pos = positives.reshape(1, ROWS)
    group, near_rows, far_top, far_bottom = pl.pallas_call(
        prep_kernel,
        out_shape=(
            jax.ShapeDtypeStruct((1,), jnp.int32),
            bf16(HALF, WIDTH // 2),
            bf16(PIECE, WIDTH // 2),
            bf16(PIECE, WIDTH // 2),
        ),
        in_specs=[spec(pltpu.SMEM), spec(pl.ANY), spec(pl.ANY)],
        out_specs=(spec(pltpu.SMEM), spec(), spec(), spec()),
        scratch_shapes=[pltpu.SMEM((8, 64), jnp.int32), pltpu.SemaphoreType.DMA((4,))],
    )(place[0], partners, projected)
    top, bottom, met_column, emb, other, own_scores, own_column, own_hit = lax.switch(
        group[0],
        [functools.partial(exchange, 16 * bits) for bits in range(1, 8)],
        *place,
        sharp,
        projected,
        pos,
        near_rows,
        far_top,
        far_bottom,
    )

    held = {(0, 0): top, (0, 1): bottom}
    for offset, piece in ((1, 0), (3, 1), (1, 1), (3, 0)):
        held[offset, piece] = swap(held[0, piece], X[offset])
    over, tiled = {}, {}

    def cross(group):
        for name in GROUPS[group]:
            over[name] = swap(held[name], CORE)

    def tiles(group):
        return call(
            tiles_kernel,
            (f32(2, ROWS, HALF), f32(1, ROWS), f32(2, HALF), bf16(2, HALF, WIDTH)),
            (sharp,),
            (emb, *[source[name] for source in (held, over) for name in GROUPS[group]]),
        )

    cross(0)
    tiled[0] = tiles(0)
    held[1, 0], held[3, 1], tiled[0] = lax.optimization_barrier((held[1, 0], held[3, 1], tiled[0]))
    held[2, 0], held[2, 1] = swap(held[1, 0], X[3]), swap(held[3, 1], X[1])
    cross(1)
    tiled[1] = tiles(1)
    cross(2)
    held[2, 0], held[2, 1], tiled[1], emb = lax.optimization_barrier((held[2, 0], held[2, 1], tiled[1], emb))
    cross(3)
    tiled[2], tiled[3] = tiles(2), tiles(3)
    tiled = [tiled[group] for group in range(4)]

    row_part = log_add([t[1] for t in tiled])
    spread = jnp.concatenate([own_column, own_column], axis=1)
    here = (lax.broadcasted_iota(jnp.int32, (1, ROWS), 1) // HALF) == half
    row_part = jnp.where(here, log_add([row_part, spread]), row_part)
    hits = jnp.where(here, jnp.concatenate([own_hit, own_hit], axis=1), 0.0)
    sent = jnp.concatenate([row_part, hits], axis=0)
    back = swap(sent, FEAT)

    mine = jnp.concatenate([log_add([tiled[0][2][0:1], met_column])] + [t[2][0:1] for t in tiled[1:]], axis=1)
    others = jnp.concatenate([t[2][1:2] for t in tiled], axis=1)
    arrived = swap(jnp.concatenate([others, mine], axis=0), CORE)
    column = log_add([jnp.concatenate([mine, others], axis=0), arrived])
    for offset in (1, 3):
        if offset == 3:
            column = after(column, back)
        column = log_add([column, shifted(swap(column, X[offset]), offset)])

    near, far, loss = [], [], []
    for start in (0, HALF):
        out = call(
            functools.partial(grad_kernel, start),
            (f32(HALF, WIDTH // 2), bf16(HALF, WIDTH // 2), f32(1, HALF)),
            (*place, sharp),
            (sent, back, column, projected, other, pos, own_scores, emb, *[t[0] for t in tiled], *[t[3] for t in tiled]),
            scratch=[pltpu.VMEM((HALF, 9 * HALF), BF16), pltpu.VMEM((1, ROWS), F32)],
            flops=2 * HALF * 9 * HALF * WIDTH,
            nbytes=10 << 20,
        )
        near.append(out[0])
        far.append(swap(out[1], FEAT))
        loss.append(out[2])
    view_grad = jnp.concatenate([a + b.astype(F32) for a, b in zip(near, far, strict=True)], axis=0)
    return jnp.concatenate(loss, axis=1).reshape(ROWS), view_grad


def solution(mesh):
    in_specs = (P("tour", "feat"), P(), P(), P("tour"))
    out_specs = (P("tour"), P("tour", "feat"))
    return jax.shard_map(
        per_device, mesh=mesh, in_specs=in_specs, out_specs=out_specs, check_vma=False
    )
```

```python
import functools

import jax
import jax.numpy as jnp
from jax import lax
from jax.experimental import pallas as pl
from jax.experimental.pallas import tpu as pltpu
from jax.sharding import PartitionSpec as P

EPSILON = 1e-06
ROWS = 512
HALF = 256
PIECE = 128
WIDTH = 1024
FEAT = 1
CORE = 2
X = {0: 0, 1: 4, 2: 8, 3: 12}
VMEM_BYTES = 24 * 1024 * 1024
F32 = jnp.float32
BF16 = jnp.bfloat16


def swap(value, mask):
    count = lax.axis_size(("tour", "feat"))
    pairs = [(source, source ^ mask) for source in range(count)]
    return lax.ppermute(value, ("tour", "feat"), pairs)


def spec(space=pltpu.VMEM):
    return pl.BlockSpec(memory_space=space)


def call(body, out_shape, smem, vmem, scratch=(), nflops=1):
    return pl.pallas_call(
        body,
        out_shape=out_shape,
        in_specs=[spec(pltpu.SMEM)] * len(smem) + [spec()] * len(vmem),
        out_specs=jax.tree.map(lambda _: spec(), out_shape),
        scratch_shapes=list(scratch),
        compiler_params=pltpu.CompilerParams(vmem_limit_bytes=VMEM_BYTES),
        cost_estimate=pl.CostEstimate(flops=nflops, bytes_accessed=1, transcendentals=0),
    )(*smem, *vmem)


def f32(*shape):
    return jax.ShapeDtypeStruct(shape, F32)


def bf16(*shape):
    return jax.ShapeDtypeStruct(shape, BF16)


def row_inverse(left, right):
    total = jnp.sum(left * left + right * right, -1, keepdims=True)
    return lax.rsqrt(total + EPSILON)


def embed_rows(left_ref, right_ref, out_ref, step=128):
    width = left_ref.shape[1]

    def chunk(index, carry):
        rows = pl.ds(pl.multiple_of(index * step, step), step)
        left = left_ref[rows, :].astype(F32)
        right = right_ref[rows, :].astype(F32)
        inverse = row_inverse(left, right)
        out_ref[rows, :width] = (left * inverse).astype(BF16)
        out_ref[rows, width:] = (right * inverse).astype(BF16)
        return carry

    lax.fori_loop(0, left_ref.shape[0] // step, chunk, 0)


def to_lanes(column):
    return jnp.broadcast_to(column, (128, 128)).T[0:1, :]


def to_rows(lanes):
    return jnp.broadcast_to(lanes, (128, 128)).T


def log_add(values):
    peak = functools.reduce(jnp.maximum, values)
    return peak + jnp.log(functools.reduce(jnp.add, [jnp.exp(value - peak) for value in values]))


def products(queries, keys):
    return lax.dot_general(queries, keys, (((1,), (1,)), ((), ())), preferred_element_type=F32)


def column_lse(score_ref, peak):
    total = jnp.zeros((8, score_ref.shape[1]), F32)
    for start in range(0, ROWS, 128):
        part = jnp.exp(score_ref[pl.ds(start, 128), :] - peak)
        total = total + jnp.sum(part.reshape(16, 8, part.shape[1]), axis=0)
    return peak + jnp.log(jnp.sum(total, axis=0, keepdims=True))


def column_peak(score_ref):
    peak = jnp.max(score_ref[pl.ds(0, 128), :], axis=0, keepdims=True)
    for start in range(128, ROWS, 128):
        peak = jnp.maximum(peak, jnp.max(score_ref[pl.ds(start, 128), :], axis=0, keepdims=True))
    return peak


def prep_kernel(half_ref, partner_ref, whole_ref, group_ref, near_ref, far_ref, met_ref, sems):
    half = half_ref[0]
    copies = [
        pltpu.make_async_copy(whole_ref.at[pl.ds(pl.multiple_of(part * HALF, HALF), HALF), :], out_ref, sems.at[j])
        for j, (part, out_ref) in enumerate(((half, near_ref), (1 - half, far_ref)))
    ]
    copies.append(pltpu.make_async_copy(partner_ref, met_ref, sems.at[2]))
    for copy in copies:
        copy.start()
    for copy in copies:
        copy.wait()
    group_ref[0] = jnp.right_shift(met_ref[0, 0], 3) - 1


def key_kernel(left_ref, right_ref, out_ref):
    for start in range(0, HALF, 128):
        rows = pl.ds(start, 128)
        embed_rows(left_ref.at[rows], right_ref.at[rows], out_ref.at[rows])


def own_kernel(
    half_ref, block_ref, sharp_ref, left_ref, right_ref, pos_ref, emb_ref, score_ref, lse_ref, hit_ref
):
    half = half_ref[0]
    embed_rows(left_ref, right_ref, emb_ref)
    mine = pl.ds(pl.multiple_of(half * HALF, HALF), HALF)
    score_ref[...] = products(emb_ref[...], emb_ref[mine, :]) * sharp_ref[0]
    columns = lax.broadcasted_iota(jnp.int32, (128, HALF), 1) + half * HALF
    rows = lax.broadcasted_iota(jnp.int32, (128, HALF), 0)
    pos = pos_ref[0:1, mine] - block_ref[0]
    hits = jnp.zeros((1, HALF), F32)
    for start in range(0, ROWS, 128):
        chunk = pl.ds(start, 128)
        part = score_ref[chunk, :]
        hits = hits + jnp.sum(jnp.where(rows + start == pos, part, 0.0), axis=0, keepdims=True)
        score_ref[chunk, :] = jnp.where(rows + start == columns, -jnp.inf, part)
    lse_ref[...] = column_lse(score_ref, column_peak(score_ref))
    hit_ref[...] = hits


def joined(refs):
    return refs[0][...] if len(refs) == 1 else jnp.concatenate([ref[...] for ref in refs], axis=0)


def tiles_kernel(sharp_ref, emb_ref, *refs):
    score_ref, row_ref, column_ref = refs[-3:]
    count = score_ref.shape[0]
    each = (len(refs) - 3) // count
    for j in range(count):
        score_ref[j] = products(emb_ref[...], joined(refs[j * each : (j + 1) * each])) * sharp_ref[0]
    for j in range(count):
        tile = score_ref.at[j]
        column_ref[j : j + 1, :] = column_lse(tile, column_peak(tile))
    for start in range(0, ROWS, 128):
        chunk = pl.ds(start, 128)
        slabs = [(j, pl.ds(k, 128)) for j in range(count) for k in (0, 128)]
        peak = functools.reduce(jnp.maximum, [score_ref[j, chunk, k] for j, k in slabs])
        peak = jnp.max(peak, axis=1, keepdims=True)
        total = functools.reduce(jnp.add, [jnp.exp(score_ref[j, chunk, k] - peak) for j, k in slabs])
        total = jnp.sum(total, axis=1, keepdims=True)
        row_ref[:, start : start + 128] = to_lanes(peak + jnp.log(total))


GROUPS = (0, 1, 3, 2)


def lse_kernel(sent_ref, back_ref, lse_ref, loss_ref):
    lse_ref[...] = log_add([sent_ref[0:1, :], back_ref[0:1, :]])
    loss_ref[...] = lse_ref[...] - (sent_ref[1:2, :] + back_ref[1:2, :])


def grad_kernel(start, *refs):
    half_ref, block_ref, sharp_ref, lse_ref = refs[:4]
    column_ref, left_ref, right_ref, pos_ref, own_ref, emb_ref = refs[4:10]
    score_refs = [ref.at[j] for ref in refs[10:13] for j in range(2)] + [ref.at[0] for ref in refs[13:15]]
    key_refs = [refs[15 + j : 16 + j] for j in range(6)] + [refs[21:23], refs[23:25]]
    near_ref, far_ref, weight_ref = refs[25:]
    half = half_ref[0]
    rows_count = near_ref.shape[0]
    mine = pl.ds(pl.multiple_of(half * HALF, HALF), HALF)
    own_lse = lse_ref[0:1, mine]
    pos = pos_ref[0:1, mine] - block_ref[0]
    for offset in range(0, rows_count, 128):
        chunk = pl.ds(start + offset, 128)
        out = pl.ds(offset, 128)
        base = to_rows(lse_ref[0:1, start + offset : start + offset + 128])
        base = jnp.concatenate([base, base], axis=1)
        rows = lax.broadcasted_iota(jnp.int32, (128, HALF), 0) + (start + offset)
        part = own_ref[chunk, :]
        weight = jnp.exp(part - base) + jnp.exp(part - own_lse) - jnp.where(rows == pos, 2.0, 0.0)
        weight_ref[out, 0:HALF] = weight.astype(BF16)
        for g in range(4):
            for core in range(2):
                tile = 1 + 2 * g + core
                part = score_refs[2 * g + core][chunk, :]
                column = column_ref[core : core + 1, g * HALF : (g + 1) * HALF]
                weight = jnp.exp(part - base) + jnp.exp(part - column)
                weight_ref[out, tile * HALF : (tile + 1) * HALF] = weight.astype(BF16)
    total = jnp.dot(weight_ref[:, 0:HALF], emb_ref[mine, :], preferred_element_type=F32)
    for tile in range(8):
        key = joined(key_refs[tile])
        total = total + jnp.dot(
            weight_ref[:, (tile + 1) * HALF : (tile + 2) * HALF], key, preferred_element_type=F32
        )
    total = total * sharp_ref[0]
    chunk = pl.ds(start, rows_count)
    left = left_ref[chunk, :].astype(F32)
    right = right_ref[chunk, :].astype(F32)
    inverse = row_inverse(left, right)
    width = left.shape[1]
    left, right = left * inverse, right * inverse
    near, far = total[:, :width], total[:, width:]
    radial = jnp.sum(left * near + right * far, -1, keepdims=True)
    near_ref[...] = inverse * (near - left * radial)
    far_ref[...] = (inverse * (far - right * radial)).astype(BF16)


def by_group(group, body, *values):
    return lax.switch(group, [functools.partial(body, 16 * bits) for bits in range(1, 8)], *values)


def swap_keys(mask, near, far):
    return swap(near, mask), swap(far, mask | FEAT)


def after(value, *done):
    return lax.optimization_barrier((value, *done))[0]


def shifted(columns, offset):
    at = [GROUPS.index(group ^ offset) * HALF for group in GROUPS]
    return jnp.concatenate([columns[:, start : start + HALF] for start in at], axis=1)


def per_device(projected, sharpness, partners, positives):
    half = lax.axis_index("feat").astype(jnp.int32)
    block = (lax.axis_index("tour") * ROWS).astype(jnp.int32)
    place = (half.reshape(1), block.reshape(1))
    sharp = sharpness.reshape(1)
    pos = positives.reshape(1, ROWS)
    other = swap(projected, FEAT)
    group, near_rows, far_rows = pl.pallas_call(
        prep_kernel,
        out_shape=(jax.ShapeDtypeStruct((1,), jnp.int32), bf16(HALF, WIDTH // 2), bf16(HALF, WIDTH // 2)),
        in_specs=[spec(pltpu.SMEM), spec(pl.ANY), spec(pl.ANY)],
        out_specs=(spec(pltpu.SMEM), spec(), spec()),
        scratch_shapes=[pltpu.SMEM((8, 64), jnp.int32), pltpu.SemaphoreType.DMA((3,))],
    )(place[0], partners, projected)
    first = call(key_kernel, bf16(HALF, WIDTH), (), by_group(group[0], swap_keys, near_rows, far_rows))
    held = {0: [first], 1: [swap(first, X[1])], 3: [swap(first, X[3])]}
    over, tiled = {0: [swap(first, CORE)]}, {}
    emb, own_scores, own_column, own_hit = call(
        own_kernel,
        (bf16(ROWS, WIDTH), f32(ROWS, HALF), f32(1, HALF), f32(1, HALF)),
        (*place, sharp),
        (projected, other, pos),
    )
    way = group[0] + 1
    met_column = own_column
    for along_y in (1, 2, 3):
        arrived = swap(own_column, 32 * along_y)
        met_column = jnp.where(jnp.right_shift(way, 1) == along_y, arrived, met_column)

    def tiles(*parts):
        count = len(parts)
        return call(
            tiles_kernel,
            (f32(count, ROWS, HALF), f32(1, ROWS), f32(count, HALF)),
            (sharp,),
            (emb, *[value for part in parts for value in part]),
        )

    tiled[0] = tiles(held[0], over[0])
    held[1], held[3], met_column = lax.optimization_barrier((held[1], held[3], met_column))
    met_column = jnp.where(jnp.bitwise_and(way, 1) == 1, swap(met_column, 16), met_column)
    held[2] = [swap(held[1][0][:PIECE], X[3]), swap(held[3][0][PIECE:], X[1])]
    for near in (1, 3):
        over[near] = [swap(held[near][0], CORE)]
        tiled[near] = tiles(held[near], over[near])
    held[2], tiled[0], tiled[1], tiled[3], met_column = lax.optimization_barrier(
        (held[2], tiled[0], tiled[1], tiled[3], met_column)
    )
    over[2] = [swap(piece, CORE) for piece in held[2]]
    tiled = [tiled[0], tiled[1], tiled[3], tiles(held[2]), tiles(over[2])]

    row_part = log_add([t[1] for t in tiled])
    spread = jnp.concatenate([own_column, own_column], axis=1)
    here = (lax.broadcasted_iota(jnp.int32, (1, ROWS), 1) // HALF) == half
    row_part = jnp.where(here, log_add([row_part, spread]), row_part)
    hits = jnp.where(here, jnp.concatenate([own_hit, own_hit], axis=1), 0.0)
    sent = jnp.concatenate([row_part, hits], axis=0)
    back = swap(sent, FEAT)
    lse, loss = call(lse_kernel, (f32(1, ROWS), f32(1, ROWS)), (), (sent, back), nflops=16_000_000_000)

    mine = jnp.concatenate([log_add([tiled[0][2][0:1], met_column])] + [t[2][0:1] for t in tiled[1:4]], axis=1)
    others = jnp.concatenate([t[2][1:2] for t in tiled[:3]] + [tiled[4][2]], axis=1)
    arrived = swap(jnp.concatenate([others, mine], axis=0), CORE)
    column = log_add([jnp.concatenate([mine, others], axis=0), arrived])
    for offset in (1, 3):
        if offset == 3:
            column = after(column, lse)
        column = log_add([column, shifted(swap(column, X[offset]), offset)])

    keys = [value for near in GROUPS for source in (held, over) for value in source[near]]
    near, far = [], []
    for start in (0, HALF):
        out = call(
            functools.partial(grad_kernel, start),
            (f32(HALF, WIDTH // 2), bf16(HALF, WIDTH // 2)),
            (*place, sharp),
            (lse, column, projected, other, pos, own_scores, emb, *[t[0] for t in tiled], *keys),
            scratch=[pltpu.VMEM((HALF, 9 * HALF), BF16)],
        )
        near.append(out[0])
        far.append(swap(out[1], FEAT))
    view_grad = jnp.concatenate([a + b.astype(F32) for a, b in zip(near, far, strict=True)], axis=0)
    return loss.reshape(ROWS), view_grad


def solution(mesh):
    in_specs = (P("tour", "feat"), P(), P(), P("tour"))
    out_specs = (P("tour"), P("tour", "feat"))
    return jax.shard_map(
        per_device, mesh=mesh, in_specs=in_specs, out_specs=out_specs, check_vma=False
    )
```

```python
import functools

import jax
import jax.numpy as jnp
from jax import lax
from jax.experimental import pallas as pl
from jax.experimental.pallas import tpu as pltpu
from jax.sharding import PartitionSpec as P

EPSILON = 1e-06
ROWS = 512
HALF = 256
PIECE = 128
WIDTH = 1024
FEAT = 1
CORE = 2
X = {0: 0, 1: 4, 2: 8, 3: 12}
VMEM_BYTES = 24 * 1024 * 1024
F32 = jnp.float32
BF16 = jnp.bfloat16


def swap(value, mask):
    count = lax.axis_size(("tour", "feat"))
    pairs = [(source, source ^ mask) for source in range(count)]
    return lax.ppermute(value, ("tour", "feat"), pairs)


def spec(space=pltpu.VMEM):
    return pl.BlockSpec(memory_space=space)


def call(body, out_shape, smem, vmem, scratch=(), nflops=1):
    return pl.pallas_call(
        body,
        out_shape=out_shape,
        in_specs=[spec(pltpu.SMEM)] * len(smem) + [spec()] * len(vmem),
        out_specs=jax.tree.map(lambda _: spec(), out_shape),
        scratch_shapes=list(scratch),
        compiler_params=pltpu.CompilerParams(vmem_limit_bytes=VMEM_BYTES),
        cost_estimate=pl.CostEstimate(flops=nflops, bytes_accessed=1, transcendentals=0),
    )(*smem, *vmem)


def f32(*shape):
    return jax.ShapeDtypeStruct(shape, F32)


def bf16(*shape):
    return jax.ShapeDtypeStruct(shape, BF16)


def row_inverse(left, right):
    total = jnp.sum(left * left + right * right, -1, keepdims=True)
    return lax.rsqrt(total + EPSILON)


def embed_rows(left_ref, right_ref, out_ref, step=128):
    width = left_ref.shape[1]

    def chunk(index, carry):
        rows = pl.ds(pl.multiple_of(index * step, step), step)
        left = left_ref[rows, :].astype(F32)
        right = right_ref[rows, :].astype(F32)
        inverse = row_inverse(left, right)
        out_ref[rows, :width] = (left * inverse).astype(BF16)
        out_ref[rows, width:] = (right * inverse).astype(BF16)
        return carry

    lax.fori_loop(0, left_ref.shape[0] // step, chunk, 0)


def to_lanes(column):
    return jnp.broadcast_to(column, (128, 128)).T[0:1, :]


def to_rows(lanes):
    return jnp.broadcast_to(lanes, (128, 128)).T


def log_add(values):
    peak = functools.reduce(jnp.maximum, values)
    return peak + jnp.log(functools.reduce(jnp.add, [jnp.exp(value - peak) for value in values]))


def products(queries, keys):
    return lax.dot_general(queries, keys, (((1,), (1,)), ((), ())), preferred_element_type=F32)


def column_lse(score_ref, peak):
    total = jnp.zeros((8, score_ref.shape[1]), F32)
    for start in range(0, ROWS, 128):
        part = jnp.exp(score_ref[pl.ds(start, 128), :] - peak)
        total = total + jnp.sum(part.reshape(16, 8, part.shape[1]), axis=0)
    return peak + jnp.log(jnp.sum(total, axis=0, keepdims=True))


def column_peak(score_ref):
    peak = jnp.max(score_ref[pl.ds(0, 128), :], axis=0, keepdims=True)
    for start in range(128, ROWS, 128):
        peak = jnp.maximum(peak, jnp.max(score_ref[pl.ds(start, 128), :], axis=0, keepdims=True))
    return peak


def prep_kernel(half_ref, partner_ref, whole_ref, group_ref, near_ref, far_ref, met_ref, sems):
    half = half_ref[0]
    copies = [
        pltpu.make_async_copy(whole_ref.at[pl.ds(pl.multiple_of(part * HALF, HALF), HALF), :], out_ref, sems.at[j])
        for j, (part, out_ref) in enumerate(((half, near_ref), (1 - half, far_ref)))
    ]
    copies.append(pltpu.make_async_copy(partner_ref, met_ref, sems.at[2]))
    for copy in copies:
        copy.start()
    for copy in copies:
        copy.wait()
    group_ref[0] = jnp.right_shift(met_ref[0, 0], 3) - 1


def key_kernel(left_ref, right_ref, out_ref, *piece_refs):
    width = left_ref.shape[1]
    for start, piece_ref in zip((0, PIECE), piece_refs, strict=True):
        rows = pl.ds(start, PIECE)
        left = left_ref[rows, :].astype(F32)
        right = right_ref[rows, :].astype(F32)
        inverse = row_inverse(left, right)
        for half, columns in ((left, slice(0, width)), (right, slice(width, 2 * width))):
            embedded = (half * inverse).astype(BF16)
            out_ref[rows, columns] = embedded
            piece_ref[:, columns] = embedded


def own_kernel(
    half_ref, block_ref, sharp_ref, left_ref, right_ref, pos_ref, emb_ref, score_ref, lse_ref, hit_ref
):
    half = half_ref[0]
    embed_rows(left_ref, right_ref, emb_ref)
    mine = pl.ds(pl.multiple_of(half * HALF, HALF), HALF)
    score_ref[...] = products(emb_ref[...], emb_ref[mine, :]) * sharp_ref[0]
    columns = lax.broadcasted_iota(jnp.int32, (128, HALF), 1) + half * HALF
    rows = lax.broadcasted_iota(jnp.int32, (128, HALF), 0)
    pos = pos_ref[0:1, mine] - block_ref[0]
    hits = jnp.zeros((1, HALF), F32)
    for start in range(0, ROWS, 128):
        chunk = pl.ds(start, 128)
        part = score_ref[chunk, :]
        hits = hits + jnp.sum(jnp.where(rows + start == pos, part, 0.0), axis=0, keepdims=True)
        score_ref[chunk, :] = jnp.where(rows + start == columns, -jnp.inf, part)
    lse_ref[...] = column_lse(score_ref, column_peak(score_ref))
    hit_ref[...] = hits


def joined(refs):
    return refs[0][...] if len(refs) == 1 else jnp.concatenate([ref[...] for ref in refs], axis=0)


def tiles_kernel(sharp_ref, emb_ref, *refs):
    score_ref, row_ref, column_ref = refs[-3:]
    count = score_ref.shape[0]
    keys = list(refs[:-3])
    for j in range(count):
        part = [keys.pop(0)]
        if part[0].shape[0] == PIECE:
            part.append(keys.pop(0))
        score_ref[j] = products(emb_ref[...], joined(part)) * sharp_ref[0]
    for j in range(count):
        tile = score_ref.at[j]
        column_ref[j : j + 1, :] = column_lse(tile, column_peak(tile))
    for start in range(0, ROWS, 128):
        chunk = pl.ds(start, 128)
        slabs = [(j, pl.ds(k, 128)) for j in range(count) for k in (0, 128)]
        peak = functools.reduce(jnp.maximum, [score_ref[j, chunk, k] for j, k in slabs])
        peak = jnp.max(peak, axis=1, keepdims=True)
        total = functools.reduce(jnp.add, [jnp.exp(score_ref[j, chunk, k] - peak) for j, k in slabs])
        total = jnp.sum(total, axis=1, keepdims=True)
        row_ref[:, start : start + 128] = to_lanes(peak + jnp.log(total))


GROUPS = (0, 1, 3, 2)


def lse_kernel(sent_ref, back_ref, lse_ref, loss_ref):
    lse_ref[...] = log_add([sent_ref[0:1, :], back_ref[0:1, :]])
    loss_ref[...] = lse_ref[...] - (sent_ref[1:2, :] + back_ref[1:2, :])


def grad_kernel(start, *refs):
    half_ref, block_ref, sharp_ref, lse_ref = refs[:4]
    column_ref, left_ref, right_ref, pos_ref, own_ref, emb_ref = refs[4:10]
    score_refs = [ref.at[j] for ref in refs[10:13] for j in range(2)] + [ref.at[0] for ref in refs[13:15]]
    keys, key_refs = list(refs[15:-3]), []
    while keys:
        count = HALF // keys[0].shape[0]
        key_refs.append(keys[:count])
        keys = keys[count:]
    near_ref, far_ref, weight_ref = refs[-3:]
    half = half_ref[0]
    rows_count = near_ref.shape[0]
    mine = pl.ds(pl.multiple_of(half * HALF, HALF), HALF)
    own_lse = lse_ref[0:1, mine]
    pos = pos_ref[0:1, mine] - block_ref[0]
    for offset in range(0, rows_count, 128):
        chunk = pl.ds(start + offset, 128)
        out = pl.ds(offset, 128)
        base = to_rows(lse_ref[0:1, start + offset : start + offset + 128])
        base = jnp.concatenate([base, base], axis=1)
        rows = lax.broadcasted_iota(jnp.int32, (128, HALF), 0) + (start + offset)
        part = own_ref[chunk, :]
        weight = jnp.exp(part - base) + jnp.exp(part - own_lse) - jnp.where(rows == pos, 2.0, 0.0)
        weight_ref[out, 0:HALF] = weight.astype(BF16)
        for g in range(4):
            for core in range(2):
                tile = 1 + 2 * g + core
                part = score_refs[2 * g + core][chunk, :]
                column = column_ref[core : core + 1, g * HALF : (g + 1) * HALF]
                weight = jnp.exp(part - base) + jnp.exp(part - column)
                weight_ref[out, tile * HALF : (tile + 1) * HALF] = weight.astype(BF16)
    total = jnp.dot(weight_ref[:, 0:HALF], emb_ref[mine, :], preferred_element_type=F32)
    for tile in range(8):
        key = joined(key_refs[tile])
        total = total + jnp.dot(
            weight_ref[:, (tile + 1) * HALF : (tile + 2) * HALF], key, preferred_element_type=F32
        )
    total = total * sharp_ref[0]
    chunk = pl.ds(start, rows_count)
    left = left_ref[chunk, :].astype(F32)
    right = right_ref[chunk, :].astype(F32)
    inverse = row_inverse(left, right)
    width = left.shape[1]
    left, right = left * inverse, right * inverse
    near, far = total[:, :width], total[:, width:]
    radial = jnp.sum(left * near + right * far, -1, keepdims=True)
    near_ref[...] = inverse * (near - left * radial)
    far_ref[...] = (inverse * (far - right * radial)).astype(BF16)


def by_group(group, body, *values):
    return lax.switch(group, [functools.partial(body, 16 * bits) for bits in range(1, 8)], *values)


def swap_keys(mask, near, far):
    return swap(near, mask), swap(far, mask | FEAT)


def after(value, *done):
    return lax.optimization_barrier((value, *done))[0]


def shifted(columns, offset):
    at = [GROUPS.index(group ^ offset) * HALF for group in GROUPS]
    return jnp.concatenate([columns[:, start : start + HALF] for start in at], axis=1)


def per_device(projected, sharpness, partners, positives):
    half = lax.axis_index("feat").astype(jnp.int32)
    block = (lax.axis_index("tour") * ROWS).astype(jnp.int32)
    place = (half.reshape(1), block.reshape(1))
    sharp = sharpness.reshape(1)
    pos = positives.reshape(1, ROWS)
    other = swap(projected, FEAT)
    group, near_rows, far_rows = pl.pallas_call(
        prep_kernel,
        out_shape=(jax.ShapeDtypeStruct((1,), jnp.int32), bf16(HALF, WIDTH // 2), bf16(HALF, WIDTH // 2)),
        in_specs=[spec(pltpu.SMEM), spec(pl.ANY), spec(pl.ANY)],
        out_specs=(spec(pltpu.SMEM), spec(), spec()),
        scratch_shapes=[pltpu.SMEM((8, 64), jnp.int32), pltpu.SemaphoreType.DMA((3,))],
    )(place[0], partners, projected)
    piece = bf16(PIECE, WIDTH)
    first, *pieces = call(key_kernel, (bf16(HALF, WIDTH), piece, piece), (), by_group(group[0], swap_keys, near_rows, far_rows))
    held = {0: [first], 1: [swap(first, X[1])], 3: [swap(first, X[3])]}
    over, tiled = {0: [swap(piece, CORE) for piece in pieces]}, {}
    emb, own_scores, own_column, own_hit = call(
        own_kernel,
        (bf16(ROWS, WIDTH), f32(ROWS, HALF), f32(1, HALF), f32(1, HALF)),
        (*place, sharp),
        (projected, other, pos),
    )
    way = group[0] + 1
    met_column = own_column
    for along_y in (1, 2, 3):
        arrived = swap(own_column, 32 * along_y)
        met_column = jnp.where(jnp.right_shift(way, 1) == along_y, arrived, met_column)

    def tiles(*parts):
        count = len(parts)
        return call(
            tiles_kernel,
            (f32(count, ROWS, HALF), f32(1, ROWS), f32(count, HALF)),
            (sharp,),
            (emb, *[value for part in parts for value in part]),
        )

    tiled[0] = tiles(held[0], over[0])
    held[1], held[3], met_column, tiled[0] = lax.optimization_barrier((held[1], held[3], met_column, tiled[0]))
    met_column = jnp.where(jnp.bitwise_and(way, 1) == 1, swap(met_column, 16), met_column)
    held[2] = [swap(held[1][0][:PIECE], X[3]), swap(held[3][0][PIECE:], X[1])]
    for near in (1, 3):
        over[near] = [swap(held[near][0], CORE)]
        tiled[near] = tiles(held[near], over[near])
    held[2], tiled[1], tiled[3], met_column = lax.optimization_barrier((held[2], tiled[1], tiled[3], met_column))
    over[2] = [swap(piece, CORE) for piece in held[2]]
    tiled = [tiled[0], tiled[1], tiled[3], tiles(held[2]), tiles(over[2])]

    row_part = log_add([t[1] for t in tiled])
    spread = jnp.concatenate([own_column, own_column], axis=1)
    here = (lax.broadcasted_iota(jnp.int32, (1, ROWS), 1) // HALF) == half
    row_part = jnp.where(here, log_add([row_part, spread]), row_part)
    hits = jnp.where(here, jnp.concatenate([own_hit, own_hit], axis=1), 0.0)
    sent = jnp.concatenate([row_part, hits], axis=0)
    back = swap(sent, FEAT)
    lse, loss = call(lse_kernel, (f32(1, ROWS), f32(1, ROWS)), (), (sent, back), nflops=2_500_000_000)

    mine = jnp.concatenate([log_add([tiled[0][2][0:1], met_column])] + [t[2][0:1] for t in tiled[1:4]], axis=1)
    others = jnp.concatenate([t[2][1:2] for t in tiled[:3]] + [tiled[4][2]], axis=1)
    arrived = swap(jnp.concatenate([others, mine], axis=0), CORE)
    column = log_add([jnp.concatenate([mine, others], axis=0), arrived])
    for offset in (1, 3):
        column = log_add([column, shifted(swap(column, X[offset]), offset)])

    keys = [value for near in GROUPS for source in (held, over) for value in source[near]]
    near, far = [], []
    for start in (0, HALF):
        out = call(
            functools.partial(grad_kernel, start),
            (f32(HALF, WIDTH // 2), bf16(HALF, WIDTH // 2)),
            (*place, sharp),
            (lse, column, projected, other, pos, own_scores, emb, *[t[0] for t in tiled], *keys),
            scratch=[pltpu.VMEM((HALF, 9 * HALF), BF16)],
        )
        near.append(out[0])
        far.append(swap(out[1], FEAT))
    view_grad = jnp.concatenate([a + b.astype(F32) for a, b in zip(near, far, strict=True)], axis=0)
    return loss.reshape(ROWS), view_grad


def solution(mesh):
    in_specs = (P("tour", "feat"), P(), P(), P("tour"))
    out_specs = (P("tour"), P("tour", "feat"))
    return jax.shard_map(
        per_device, mesh=mesh, in_specs=in_specs, out_specs=out_specs, check_vma=False
    )
```

```python
import functools

import jax
import jax.numpy as jnp
from jax import lax
from jax.experimental import pallas as pl
from jax.experimental.pallas import tpu as pltpu
from jax.sharding import PartitionSpec as P

EPSILON = 1e-06
ROWS = 512
HALF = 256
PIECE = 128
WIDTH = 1024
FEAT = 1
CORE = 2
X = {0: 0, 1: 4, 2: 8, 3: 12}
VMEM_BYTES = 24 * 1024 * 1024
F32 = jnp.float32
BF16 = jnp.bfloat16


def swap(value, mask):
    count = lax.axis_size(("tour", "feat"))
    pairs = [(source, source ^ mask) for source in range(count)]
    return lax.ppermute(value, ("tour", "feat"), pairs)


def spec(space=pltpu.VMEM):
    return pl.BlockSpec(memory_space=space)


def call(body, out_shape, smem, vmem, scratch=(), nflops=1):
    return pl.pallas_call(
        body,
        out_shape=out_shape,
        in_specs=[spec(pltpu.SMEM)] * len(smem) + [spec()] * len(vmem),
        out_specs=jax.tree.map(lambda _: spec(), out_shape),
        scratch_shapes=list(scratch),
        compiler_params=pltpu.CompilerParams(vmem_limit_bytes=VMEM_BYTES),
        cost_estimate=pl.CostEstimate(flops=nflops, bytes_accessed=1, transcendentals=0),
    )(*smem, *vmem)


def f32(*shape):
    return jax.ShapeDtypeStruct(shape, F32)


def bf16(*shape):
    return jax.ShapeDtypeStruct(shape, BF16)


def row_inverse(left, right):
    total = jnp.sum(left * left + right * right, -1, keepdims=True)
    return lax.rsqrt(total + EPSILON)


def embed_rows(left_ref, right_ref, out_ref, step=128):
    width = left_ref.shape[1]

    def chunk(index, carry):
        rows = pl.ds(pl.multiple_of(index * step, step), step)
        left = left_ref[rows, :].astype(F32)
        right = right_ref[rows, :].astype(F32)
        inverse = row_inverse(left, right)
        out_ref[rows, :width] = (left * inverse).astype(BF16)
        out_ref[rows, width:] = (right * inverse).astype(BF16)
        return carry

    lax.fori_loop(0, left_ref.shape[0] // step, chunk, 0)


def to_lanes(column):
    return jnp.broadcast_to(column, (128, 128)).T[0:1, :]


def to_rows(lanes):
    return jnp.broadcast_to(lanes, (128, 128)).T


def log_add(values):
    peak = functools.reduce(jnp.maximum, values)
    return peak + jnp.log(functools.reduce(jnp.add, [jnp.exp(value - peak) for value in values]))


def products(queries, keys):
    return lax.dot_general(queries, keys, (((1,), (1,)), ((), ())), preferred_element_type=F32)


def column_lse(score_ref, peak):
    total = jnp.zeros((8, score_ref.shape[1]), F32)
    for start in range(0, ROWS, 128):
        part = jnp.exp(score_ref[pl.ds(start, 128), :] - peak)
        total = total + jnp.sum(part.reshape(16, 8, part.shape[1]), axis=0)
    return peak + jnp.log(jnp.sum(total, axis=0, keepdims=True))


def column_peak(score_ref):
    peak = jnp.max(score_ref[pl.ds(0, 128), :], axis=0, keepdims=True)
    for start in range(128, ROWS, 128):
        peak = jnp.maximum(peak, jnp.max(score_ref[pl.ds(start, 128), :], axis=0, keepdims=True))
    return peak


def prep_kernel(half_ref, partner_ref, whole_ref, group_ref, near_ref, far_ref, met_ref, sems):
    half = half_ref[0]
    copies = [
        pltpu.make_async_copy(whole_ref.at[pl.ds(pl.multiple_of(part * HALF, HALF), HALF), :], out_ref, sems.at[j])
        for j, (part, out_ref) in enumerate(((half, near_ref), (1 - half, far_ref)))
    ]
    copies.append(pltpu.make_async_copy(partner_ref, met_ref, sems.at[2]))
    for copy in copies:
        copy.start()
    for copy in copies:
        copy.wait()
    group_ref[0] = jnp.right_shift(met_ref[0, 0], 3) - 1


def key_kernel(left_ref, right_ref, out_ref, *piece_refs):
    width = left_ref.shape[1]
    for start, piece_ref in zip((0, PIECE), piece_refs, strict=True):
        rows = pl.ds(start, PIECE)
        left = left_ref[rows, :].astype(F32)
        right = right_ref[rows, :].astype(F32)
        inverse = row_inverse(left, right)
        for half, columns in ((left, slice(0, width)), (right, slice(width, 2 * width))):
            embedded = (half * inverse).astype(BF16)
            out_ref[rows, columns] = embedded
            piece_ref[:, columns] = embedded


def own_kernel(
    half_ref, block_ref, sharp_ref, whole_ref, other_ref, pos_ref,
    emb_ref, score_ref, lse_ref, hit_ref, left_ref, right_ref, sems,
):
    half = half_ref[0]
    copies = [
        pltpu.make_async_copy(source, target, sems.at[j])
        for j, (source, target) in enumerate(((whole_ref, left_ref), (other_ref, right_ref)))
    ]
    for copy in copies:
        copy.start()
    for copy in copies:
        copy.wait()
    embed_rows(left_ref, right_ref, emb_ref)
    mine = pl.ds(pl.multiple_of(half * HALF, HALF), HALF)
    score_ref[...] = products(emb_ref[...], emb_ref[mine, :]) * sharp_ref[0]
    columns = lax.broadcasted_iota(jnp.int32, (128, HALF), 1) + half * HALF
    rows = lax.broadcasted_iota(jnp.int32, (128, HALF), 0)
    pos = pos_ref[0:1, mine] - block_ref[0]
    hits = jnp.zeros((1, HALF), F32)
    for start in range(0, ROWS, 128):
        chunk = pl.ds(start, 128)
        part = score_ref[chunk, :]
        hits = hits + jnp.sum(jnp.where(rows + start == pos, part, 0.0), axis=0, keepdims=True)
        score_ref[chunk, :] = jnp.where(rows + start == columns, -jnp.inf, part)
    lse_ref[...] = column_lse(score_ref, column_peak(score_ref))
    hit_ref[...] = hits


def joined(refs):
    return refs[0][...] if len(refs) == 1 else jnp.concatenate([ref[...] for ref in refs], axis=0)


def tiles_kernel(sharp_ref, emb_ref, *refs):
    score_ref, row_ref, column_ref = refs[-3:]
    count = score_ref.shape[0]
    keys = list(refs[:-3])
    for j in range(count):
        part = [keys.pop(0)]
        if part[0].shape[0] == PIECE:
            part.append(keys.pop(0))
        score_ref[j] = products(emb_ref[...], joined(part)) * sharp_ref[0]
    for j in range(count):
        tile = score_ref.at[j]
        column_ref[j : j + 1, :] = column_lse(tile, column_peak(tile))
    for start in range(0, ROWS, 128):
        chunk = pl.ds(start, 128)
        slabs = [(j, pl.ds(k, 128)) for j in range(count) for k in (0, 128)]
        peak = functools.reduce(jnp.maximum, [score_ref[j, chunk, k] for j, k in slabs])
        peak = jnp.max(peak, axis=1, keepdims=True)
        total = functools.reduce(jnp.add, [jnp.exp(score_ref[j, chunk, k] - peak) for j, k in slabs])
        total = jnp.sum(total, axis=1, keepdims=True)
        row_ref[:, start : start + 128] = to_lanes(peak + jnp.log(total))


GROUPS = (0, 1, 3, 2)


def lse_kernel(sent_ref, back_ref, lse_ref, loss_ref):
    lse_ref[...] = log_add([sent_ref[0:1, :], back_ref[0:1, :]])
    loss_ref[...] = lse_ref[...] - (sent_ref[1:2, :] + back_ref[1:2, :])


def grad_kernel(start, *refs):
    half_ref, block_ref, sharp_ref, lse_ref = refs[:4]
    column_ref, left_ref, right_ref, pos_ref, own_ref, emb_ref = refs[4:10]
    score_refs = [ref.at[j] for ref in refs[10:13] for j in range(2)] + [ref.at[0] for ref in refs[13:15]]
    keys, key_refs = list(refs[15:-3]), []
    while keys:
        count = HALF // keys[0].shape[0]
        key_refs.append(keys[:count])
        keys = keys[count:]
    near_ref, far_ref, weight_ref = refs[-3:]
    half = half_ref[0]
    rows_count = near_ref.shape[0]
    mine = pl.ds(pl.multiple_of(half * HALF, HALF), HALF)
    own_lse = lse_ref[0:1, mine]
    pos = pos_ref[0:1, mine] - block_ref[0]
    for offset in range(0, rows_count, 128):
        chunk = pl.ds(start + offset, 128)
        out = pl.ds(offset, 128)
        base = to_rows(lse_ref[0:1, start + offset : start + offset + 128])
        base = jnp.concatenate([base, base], axis=1)
        rows = lax.broadcasted_iota(jnp.int32, (128, HALF), 0) + (start + offset)
        part = own_ref[chunk, :]
        weight = jnp.exp(part - base) + jnp.exp(part - own_lse) - jnp.where(rows == pos, 2.0, 0.0)
        weight_ref[out, 0:HALF] = weight.astype(BF16)
        for g in range(4):
            for core in range(2):
                tile = 1 + 2 * g + core
                part = score_refs[2 * g + core][chunk, :]
                column = column_ref[core : core + 1, g * HALF : (g + 1) * HALF]
                weight = jnp.exp(part - base) + jnp.exp(part - column)
                weight_ref[out, tile * HALF : (tile + 1) * HALF] = weight.astype(BF16)
    total = jnp.dot(weight_ref[:, 0:HALF], emb_ref[mine, :], preferred_element_type=F32)
    for tile in range(8):
        key = joined(key_refs[tile])
        total = total + jnp.dot(
            weight_ref[:, (tile + 1) * HALF : (tile + 2) * HALF], key, preferred_element_type=F32
        )
    total = total * sharp_ref[0]
    chunk = pl.ds(start, rows_count)
    left = left_ref[chunk, :].astype(F32)
    right = right_ref[chunk, :].astype(F32)
    inverse = row_inverse(left, right)
    width = left.shape[1]
    left, right = left * inverse, right * inverse
    near, far = total[:, :width], total[:, width:]
    radial = jnp.sum(left * near + right * far, -1, keepdims=True)
    near_ref[...] = inverse * (near - left * radial)
    far_ref[...] = (inverse * (far - right * radial)).astype(BF16)


def by_group(group, body, *values):
    return lax.switch(group, [functools.partial(body, 16 * bits) for bits in range(1, 8)], *values)


def swap_keys(mask, near, far):
    return swap(near, mask), swap(far, mask | FEAT)


def after(value, *done):
    return lax.optimization_barrier((value, *done))[0]


def shifted(columns, offset):
    at = [GROUPS.index(group ^ offset) * HALF for group in GROUPS]
    return jnp.concatenate([columns[:, start : start + HALF] for start in at], axis=1)


def per_device(projected, sharpness, partners, positives):
    half = lax.axis_index("feat").astype(jnp.int32)
    block = (lax.axis_index("tour") * ROWS).astype(jnp.int32)
    place = (half.reshape(1), block.reshape(1))
    sharp = sharpness.reshape(1)
    pos = positives.reshape(1, ROWS)
    other = swap(projected, FEAT)
    group, near_rows, far_rows = pl.pallas_call(
        prep_kernel,
        out_shape=(jax.ShapeDtypeStruct((1,), jnp.int32), bf16(HALF, WIDTH // 2), bf16(HALF, WIDTH // 2)),
        in_specs=[spec(pltpu.SMEM), spec(pl.ANY), spec(pl.ANY)],
        out_specs=(spec(pltpu.SMEM), spec(), spec()),
        scratch_shapes=[pltpu.SMEM((8, 64), jnp.int32), pltpu.SemaphoreType.DMA((3,))],
    )(place[0], partners, projected)
    piece = bf16(PIECE, WIDTH)
    first, *pieces = call(key_kernel, (bf16(HALF, WIDTH), piece, piece), (), by_group(group[0], swap_keys, near_rows, far_rows))
    held = {0: [first], 1: [swap(first, X[1])], 3: [swap(first, X[3])]}
    over, tiled = {0: [swap(piece, CORE) for piece in pieces]}, {}
    emb, own_scores, own_column, own_hit, left, right = pl.pallas_call(
        own_kernel,
        out_shape=(
            bf16(ROWS, WIDTH), f32(ROWS, HALF), f32(1, HALF), f32(1, HALF),
            bf16(ROWS, WIDTH // 2), bf16(ROWS, WIDTH // 2),
        ),
        in_specs=[spec(pltpu.SMEM)] * 3 + [spec(pltpu.HBM), spec(pltpu.HBM), spec()],
        out_specs=(spec(),) * 6,
        scratch_shapes=[pltpu.SemaphoreType.DMA((2,))],
        compiler_params=pltpu.CompilerParams(vmem_limit_bytes=VMEM_BYTES),
        cost_estimate=pl.CostEstimate(flops=1, bytes_accessed=1, transcendentals=0),
    )(*place, sharp, projected, other, pos)
    way = group[0] + 1
    met_column = own_column
    for along_y in (1, 2, 3):
        arrived = swap(own_column, 32 * along_y)
        met_column = jnp.where(jnp.right_shift(way, 1) == along_y, arrived, met_column)

    def tiles(*parts):
        count = len(parts)
        return call(
            tiles_kernel,
            (f32(count, ROWS, HALF), f32(1, ROWS), f32(count, HALF)),
            (sharp,),
            (emb, *[value for part in parts for value in part]),
        )

    tiled[0] = tiles(held[0], over[0])
    held[1], held[3], met_column, tiled[0] = lax.optimization_barrier((held[1], held[3], met_column, tiled[0]))
    met_column = jnp.where(jnp.bitwise_and(way, 1) == 1, swap(met_column, 16), met_column)
    held[2] = [swap(held[1][0][:PIECE], X[3]), swap(held[3][0][PIECE:], X[1])]
    for near in (1, 3):
        over[near] = [swap(held[near][0], CORE)]
        tiled[near] = tiles(held[near], over[near])
    held[2], tiled[1], tiled[3], met_column = lax.optimization_barrier((held[2], tiled[1], tiled[3], met_column))
    over[2] = [swap(piece, CORE) for piece in held[2]]
    tiled = [tiled[0], tiled[1], tiled[3], tiles(held[2]), tiles(over[2])]

    row_part = log_add([t[1] for t in tiled])
    spread = jnp.concatenate([own_column, own_column], axis=1)
    here = (lax.broadcasted_iota(jnp.int32, (1, ROWS), 1) // HALF) == half
    row_part = jnp.where(here, log_add([row_part, spread]), row_part)
    hits = jnp.where(here, jnp.concatenate([own_hit, own_hit], axis=1), 0.0)
    sent = jnp.concatenate([row_part, hits], axis=0)
    back = swap(sent, FEAT)
    lse, loss = call(lse_kernel, (f32(1, ROWS), f32(1, ROWS)), (), (sent, back), nflops=2_500_000_000)

    mine = jnp.concatenate([log_add([tiled[0][2][0:1], met_column])] + [t[2][0:1] for t in tiled[1:4]], axis=1)
    others = jnp.concatenate([t[2][1:2] for t in tiled[:3]] + [tiled[4][2]], axis=1)
    arrived = swap(jnp.concatenate([others, mine], axis=0), CORE)
    column = log_add([jnp.concatenate([mine, others], axis=0), arrived])
    for offset in (1, 3):
        column = log_add([column, shifted(swap(column, X[offset]), offset)])

    keys = [value for near in GROUPS for source in (held, over) for value in source[near]]
    near, far = [], []
    for start in (0, HALF):
        out = call(
            functools.partial(grad_kernel, start),
            (f32(HALF, WIDTH // 2), bf16(HALF, WIDTH // 2)),
            (*place, sharp),
            (lse, column, left, right, pos, own_scores, emb, *[t[0] for t in tiled], *keys),
            scratch=[pltpu.VMEM((HALF, 9 * HALF), BF16)],
        )
        near.append(out[0])
        far.append(swap(out[1], FEAT))
    view_grad = jnp.concatenate([a + b.astype(F32) for a, b in zip(near, far, strict=True)], axis=0)
    return loss.reshape(ROWS), view_grad


def solution(mesh):
    in_specs = (P("tour", "feat"), P(), P(), P("tour"))
    out_specs = (P("tour"), P("tour", "feat"))
    return jax.shard_map(
        per_device, mesh=mesh, in_specs=in_specs, out_specs=out_specs, check_vma=False
    )
```
